32 devices in a mesh: own: 4 (over y, x), dp: 8 (over z, core).
Axes of the slice: x: 2, y: 2, z: 4, core: 2. Of those that a mesh axis runs over, the one named last changes fastest.
Arguments:
- tokens: bfloat16 [8192, 1536], P('dp'), may hold values from -6 to 6
- assign: int32 [64, 2], P('dp'), may hold values from 0 to 7, all different within a row; in each aligned block of 8 rows (0 to 7, 8 to 15, ...) at most 5 rows name the same one
- gates: float32 [8192, 2], P('dp'), may hold values from 0.25 to 1
- cot: bfloat16 [8192, 1536], P('dp', 'own'), may hold values from -1.75 to 1.75
- w_in: bfloat16 [8, 1536, 2048], P('own', None, 'dp'), may hold values from -0.15625 to 0.15625
- w_out: bfloat16 [8, 2048, 1536], P('own', 'dp'), may hold values from -0.125 to 0.125
Outputs:
- mixed: bfloat16 [8192, 1536], P('dp', 'own')
- grad_tokens: bfloat16 [8192, 1536], P('dp', 'own')
- grad_w_in: float32 [8, 1536, 2048], P('own', None, 'dp')
- grad_w_out: float32 [8, 2048, 1536], P('own', 'dp')
The draws below stay inside these ranges and needn't reach their ends.
Inputs may be any that keep to these rules, and one draw needn't show every extreme that they name: `assign`: the two entries of a block name different experts. Among the 8 blocks of one index of dp no expert is named more than 5 times, and in every draw some expert is named exactly 5 times by the blocks of some index of dp.
All inputs are finite; a program needn't handle non-finite values.
Results may differ from the reference program's by a relative error of at most 0.012.
Values may be sent and summed in bfloat16 or wider, within the bound.
A program may use at most 128 MiB of HBM per device.

```python
import math
import jax
import jax.numpy as jnp
import numpy as np
from jax import lax

D = 1536
FF = 2048
EXPERTS = 8
BLOCK = 128
BLK_DEV = 8
CAP = 5
BLOCKS = 64
TOKENS = 8192
N_OWN = 4
N_DP = 8


def levels(key, shape, cuts, smallest, largest):
    gain, own = 1.0, jax.random.fold_in(key, 6)
    for position, shards_of in cuts:
        heights = jnp.exp(jax.random.uniform(jax.random.fold_in(own, position), (shards_of,), jnp.float32, smallest / len(cuts), largest / len(cuts)))
        gain = gain * jnp.repeat(heights, shape[position] // shards_of).reshape([-1 if axis == position else 1 for axis in range(len(shape))])
    return gain


def shared_out(key, own, number, rows, count, top, reach, lean):
    sequence = jax.random.permutation(key, count)
    packed, ordinary = portions_of(count, rows * top, reach, lean, True), portions_of(count, rows * top, reach, lean, False)
    places = jnp.arange(count)

    def named(sizes, rotation):
        used = int((sizes > 0).sum())
        fixed = max(1, used // 4)
        shifted = fixed + (places - fixed + rotation * (used - fixed)) % max(1, count - fixed)
        return jnp.zeros((count,), jnp.int32).at[sequence[jnp.where(places < fixed, places, shifted)]].set(jnp.asarray(sizes, jnp.int32))

    sizes = jnp.where(number % 4 == 0, named(packed, number // 4), named(ordinary, number - number // 4 - 1))
    mixed = jax.random.permutation(jax.random.fold_in(own, 3), count)
    source_of, sink = mixed[0:count // 2 * 2:2], mixed[1:count // 2 * 2:2]
    room = jnp.minimum(sizes[source_of] - 1, reach - sizes[sink]) // 2
    room = jnp.where((source_of == sequence[0]) | (sink == sequence[0]) | (sizes[sink] == 0), 0, jnp.maximum(room, 0))
    shifted = jax.random.randint(jax.random.fold_in(own, 4), (count // 2,), 0, 1 << 20) % (room + 1)
    sizes = sizes.at[source_of].add(-shifted).at[sink].add(shifted)
    members = jnp.searchsorted(jnp.cumsum(sizes), jnp.arange(rows * top), side="right").astype(jnp.int32)
    table = members.reshape(top, rows).T
    table = table[jax.random.permutation(jax.random.fold_in(own, 1), rows)]
    rotation = jax.random.randint(jax.random.fold_in(own, 2), (rows, 1), 0, top)
    return jnp.take_along_axis(table, (jnp.arange(top)[None, :] + rotation) % top, axis=1)


def portions_of(amount, total, reach, lean, full):
    portions = [(1 << 20) // math.isqrt(standing ** lean) + 1 for standing in range(1, amount + 1)]
    largest = reach if full else min(reach, max(-(-total // amount), total * portions[0] // sum(portions)))
    least = 1 if total - largest >= amount - 1 else 0
    given, rest = [largest] + [least] * (amount - 1), total - largest - least * (amount - 1)
    while rest > 0:
        candidates = [i for i in range(1, amount) if given[i] < largest] or [i for i in range(1, amount) if given[i] < reach]
        pool, budget = sum([portions[i] for i in candidates]), rest
        for i in candidates:
            more = min(reach - given[i], max(1, budget * portions[i] // pool), rest)
            given[i] = given[i] + more
            rest = rest - more
    return np.array(given)


def centred(own_key, extent, deviation, limit, cuts=(), kind=jnp.bfloat16):
    gain = levels(own_key, extent, cuts, -0.22, 0.18) if cuts else 1.0
    array = jax.random.normal(own_key, extent, jnp.float32) * deviation * gain
    return jnp.minimum(jnp.maximum(array, -limit), limit).astype(kind)


def setup_inputs(seed: int = 0) -> dict:
    seeds = jax.random.split(jax.random.key(seed), 7)
    tokens = centred(seeds[0], (TOKENS, D), 1.0, 6.0, ((0, 8),))
    assign_keys = jax.random.split(jax.random.fold_in(seeds[1], 1), BLOCKS // BLK_DEV)
    assign_turns = jax.random.permutation(jax.random.fold_in(seeds[1], 3), BLOCKS // BLK_DEV)
    assign = jax.vmap(lambda own, number: shared_out(jax.random.fold_in(seeds[1], 2), own, number, BLK_DEV, EXPERTS, 2, CAP, 2))(assign_keys, assign_turns).reshape((BLOCKS, 2))
    gates = jnp.clip(0.25 + 0.75 * jax.random.uniform(seeds[2], (TOKENS, 2), jnp.float32) ** levels(seeds[2], (TOKENS, 2), ((0, 8),), -0.2, 0.2), 0.25, 1.0)
    cot = centred(seeds[3], (TOKENS, D), 0.3, 1.75, ((0, 8), (1, 4)))
    w_in = centred(seeds[4], (EXPERTS, D, FF), D ** -0.5, 0.15625, ((0, 4), (2, 8)))
    w_out = centred(seeds[5], (EXPERTS, FF, D), FF ** -0.5, 0.125, ((0, 4), (1, 8)))
    return {"tokens": tokens, "assign": assign, "gates": gates, "cot": cot, "w_in": w_in, "w_out": w_out}


def pick_blocks(assign_rows, expert, capacity):
    hit_flag = jnp.logical_or(assign_rows[:, 0] == expert, assign_rows[:, 1] == expert).astype(jnp.int32)
    slot_rank = jnp.cumsum(hit_flag) - 1
    slot_ids = jnp.arange(capacity, dtype=jnp.int32)
    matches = jnp.logical_and(hit_flag[None, :] == 1, slot_rank[None, :] == slot_ids[:, None]).astype(jnp.int32)
    where_idx = jnp.arange(assign_rows.shape[0], dtype=jnp.int32)
    blocks = jnp.sum(matches * where_idx[None, :], axis=1).astype(jnp.int32)
    is_valid = jnp.sum(matches, axis=1).astype(jnp.float32)
    return blocks, is_valid


def block_gates(assign_rows, gate_blocks, blocks, is_valid, expert):
    chosen = assign_rows[blocks]
    picked_gates = gate_blocks[blocks]
    first_hit = (chosen[:, 0] == expert).astype(jnp.float32)
    second_hit = (chosen[:, 1] == expert).astype(jnp.float32)
    mixing = picked_gates[..., 0] * first_hit[:, None] + picked_gates[..., 1] * second_hit[:, None]
    return mixing * is_valid[:, None]


def gelu_cdf(values):
    return 0.5 * (1.0 + jax.scipy.special.erf(values * 0.7071067811865476))


def gelu_slope(values):
    return gelu_cdf(values) + values * jnp.exp(-0.5 * values * values) * 0.3989422804014327


def place_rows(terms, blocks, block_count):
    block_len = terms.shape[-2]
    width = terms.shape[-1]
    zeros = jnp.zeros((block_count, block_len, width), jnp.float32)
    placed = zeros.at[blocks.reshape(-1)].add(terms.reshape(-1, block_len, width))
    return placed.reshape(block_count * block_len, width)


def owner_total(terms, blocks, block_count):
    own_count = EXPERTS // N_OWN
    grouped = terms.reshape((N_OWN, own_count * CAP) + terms.shape[2:])
    group_blocks = blocks.reshape(N_OWN, own_count * CAP)
    placed = jax.vmap(place_rows, (0, 0, None))(grouped, group_blocks, block_count)
    rounded = lax.optimization_barrier(placed.astype(jnp.bfloat16)).astype(jnp.float32)
    return jnp.sum(rounded, axis=0).astype(jnp.bfloat16)


def reference(tokens, assign, gates, cot, w_in, w_out):
    token_shards = tokens.reshape(N_DP, BLK_DEV, BLOCK, D)
    assign_shards = assign.reshape(N_DP, BLK_DEV, 2)
    gate_shards = gates.reshape(N_DP, BLK_DEV, BLOCK, 2)
    cot_shards = cot.reshape(N_DP, BLK_DEV, BLOCK, D)
    w_in32 = w_in.astype(jnp.float32)
    w_out32 = w_out.astype(jnp.float32)
    expert_ids = jnp.arange(EXPERTS, dtype=jnp.int32)

    def one_shard(carry, items):
        sum_in, sum_out = carry
        token_blocks, assign_rows, gate_blocks, cot_blocks = items
        blocks, is_valid = jax.vmap(pick_blocks, (None, 0, None))(assign_rows, expert_ids, CAP)
        mixing = jax.vmap(block_gates, (None, None, 0, 0, 0))(assign_rows, gate_blocks, blocks, is_valid, expert_ids)
        picked = token_blocks[blocks].reshape(EXPERTS, CAP * BLOCK, D)
        weight_rows = mixing.reshape(EXPERTS, CAP * BLOCK)
        pre_act = jnp.einsum('erd,edf->erf', picked.astype(jnp.float32), w_in32)
        hidden = (pre_act * gelu_cdf(pre_act)).astype(jnp.bfloat16)
        expert_out = jnp.einsum('erf,efd->erd', hidden.astype(jnp.float32), w_out32)
        contrib = (weight_rows[..., None] * expert_out).reshape(EXPERTS, CAP, BLOCK, D)
        mixed_rows = owner_total(contrib, blocks, BLK_DEV)
        cot_picked = cot_blocks[blocks].reshape(EXPERTS, CAP * BLOCK, D).astype(jnp.float32)
        grad_out = (weight_rows[..., None] * cot_picked).astype(jnp.bfloat16)
        grad_hidden = jnp.einsum('erd,efd->erf', grad_out.astype(jnp.float32), w_out32)
        grad_pre = (grad_hidden * gelu_slope(pre_act)).astype(jnp.bfloat16)
        grad_in_rows = jnp.einsum('erf,edf->erd', grad_pre.astype(jnp.float32), w_in32).reshape(EXPERTS, CAP, BLOCK, D)
        grad_rows = owner_total(grad_in_rows, blocks, BLK_DEV)
        out_part = jnp.einsum('erf,erd->efd', hidden.astype(jnp.float32), grad_out.astype(jnp.float32))
        in_part = jnp.einsum('erd,erf->edf', picked.astype(jnp.float32), grad_pre.astype(jnp.float32))
        out_part = lax.optimization_barrier(out_part.astype(jnp.bfloat16)).astype(jnp.float32)
        in_part = lax.optimization_barrier(in_part.astype(jnp.bfloat16)).astype(jnp.float32)
        return (sum_in + in_part, sum_out + out_part), (mixed_rows, grad_rows)

    start = (jnp.zeros((EXPERTS, D, FF), jnp.float32), jnp.zeros((EXPERTS, FF, D), jnp.float32))
    totals, rows = lax.scan(one_shard, start, (token_shards, assign_shards, gate_shards, cot_shards))
    mixed = rows[0].reshape(TOKENS, D)
    grad_tokens = rows[1].reshape(TOKENS, D)
    return mixed, grad_tokens, totals[0], totals[1]
```

```python
import functools

import jax
import jax.numpy as jnp
from jax import lax
from jax.experimental import pallas as pl
from jax.experimental.pallas import tpu as pltpu
from jax.sharding import PartitionSpec as P

CAP = 5
MESH = pl.DeviceIdType.MESH


def pick_blocks(assign_rows, expert, capacity):
    hit_flag = jnp.logical_or(assign_rows[:, 0] == expert, assign_rows[:, 1] == expert).astype(
        jnp.int32
    )
    slot_rank = jnp.cumsum(hit_flag) - 1
    slot_ids = jnp.arange(capacity, dtype=jnp.int32)
    matches = jnp.logical_and(
        hit_flag[None, :] == 1, slot_rank[None, :] == slot_ids[:, None]
    ).astype(jnp.int32)
    where_idx = jnp.arange(assign_rows.shape[0], dtype=jnp.int32)
    blocks = jnp.sum(matches * where_idx[None, :], axis=1)
    is_valid = jnp.sum(matches, axis=1).astype(jnp.float32)
    return (blocks, is_valid, hit_flag, slot_rank)


def block_gates(assign_rows, gate_blocks, blocks, is_valid, expert):
    chosen = assign_rows[blocks]
    picked_gates = gate_blocks[blocks]
    first_hit = (chosen[:, 0] == expert).astype(jnp.float32)
    second_hit = (chosen[:, 1] == expert).astype(jnp.float32)
    mixing = picked_gates[..., 0] * first_hit[:, None] + picked_gates[..., 1] * second_hit[:, None]
    return mixing * is_valid[:, None]


def expert_kernel(
    chips,
    x_ref,
    g_ref,
    wt_ref,
    own_w,
    y_out,
    gx_out,
    dw_out,
    w_all,
    h_all,
    p_all,
    sums,
    stage,
    ag_send,
    ag_recv,
    rs_send,
    rs_recv,
    own_sem,
    out_sem,
):
    me = lax.axis_index("dp")
    chip = me // 2
    rows, width = x_ref.shape
    depth = own_w.shape[1] // 2
    last = chips - 1
    has_left, has_right = chip > 0, chip < last

    def at_chunk(ref, q):
        return ref.at[:, pl.ds(pl.multiple_of(q * depth, depth), depth)]

    def gather_copy(q, way):
        return pltpu.make_async_remote_copy(
            src_ref=at_chunk(w_all, q),
            dst_ref=at_chunk(w_all, q),
            send_sem=ag_send.at[q, (way + 1) // 2],
            recv_sem=ag_recv.at[q],
            device_id={"dp": me + 2 * way},
            device_id_type=MESH,
        )

    def sum_copy(slot, way):
        return pltpu.make_async_remote_copy(
            src_ref=sums.at[slot],
            dst_ref=sums.at[slot],
            send_sem=rs_send.at[slot],
            recv_sem=rs_recv.at[slot],
            device_id={"dp": me + 2 * way},
            device_id_type=MESH,
        )

    own_copy = pltpu.make_async_copy(
        own_w, w_all.at[:, pl.ds(pl.multiple_of(chip * 2 * depth, depth), 2 * depth)], own_sem
    )
    own_copy.start()
    barrier = pltpu.get_barrier_semaphore()

    @pl.when(has_left)
    def _():
        pl.semaphore_signal(barrier, inc=1, device_id={"dp": me - 2}, device_id_type=MESH)

    @pl.when(has_right)
    def _():
        pl.semaphore_signal(barrier, inc=1, device_id={"dp": me + 2}, device_id_type=MESH)

    pl.semaphore_wait(barrier, has_left.astype(jnp.int32) + has_right.astype(jnp.int32))

    own_copy.wait()
    for sub in range(2):

        @pl.when(has_left)
        def _():
            gather_copy(2 * chip + sub, -1).start()

        @pl.when(has_right)
        def _():
            gather_copy(2 * chip + sub, 1).start()

    tile = rows // 2
    nt = (((1,), (1,)), ((), ()))

    def activate(q):
        cols = pl.ds(pl.multiple_of(q * depth, depth), depth)

        def step(r, carry):
            part = pl.ds(pl.multiple_of(r * tile, tile), tile)
            pre = lax.dot_general(
                x_ref[part, :], w_all[0, cols, :], nt, preferred_element_type=jnp.float32
            )
            grad_hidden = lax.dot_general(
                g_ref[part, :], w_all[1, cols, :], nt, preferred_element_type=jnp.float32
            )
            cdf = 0.5 * (1.0 + lax.erf(pre * 0.7071067811865476))
            slope = cdf + pre * jnp.exp(-0.5 * pre * pre) * 0.3989422804014327
            h_all[part, cols] = (pre * cdf).astype(jnp.bfloat16)
            p_all[part, cols] = (grad_hidden * slope).astype(jnp.bfloat16)
            return carry

        lax.fori_loop(0, 2, step, 0)

    piece = width // 3

    def weight_grads(q, emit):
        cols = pl.ds(pl.multiple_of(q * depth, depth), depth)
        for kind, left, right in ((0, p_all, x_ref), (1, h_all, g_ref)):
            turned = left[:, cols].T

            def step(k, carry):
                span = pl.ds(pl.multiple_of(k * piece, piece), piece)
                emit(
                    kind,
                    span,
                    jnp.dot(turned, right[:, span], preferred_element_type=jnp.float32),
                )
                return carry

            lax.fori_loop(0, 3, step, 0)

    def add_and_send(q, slot, way, fed):
        @pl.when(fed)
        def _():
            sum_copy(slot, way).wait_recv()

        @pl.when(jnp.logical_not(fed))
        def _():
            sums[slot] = jnp.zeros(sums.shape[1:], sums.dtype)

        def emit(kind, span, value):
            sums[slot, kind, :, span] = (
                value + sums[slot, kind, :, span].astype(jnp.float32)
            ).astype(jnp.bfloat16)

        weight_grads(q, emit)
        sum_copy(slot, way).start()

    def chunk_of(n, way):
        return 2 * (chip + way * (1 + n // 2)) + n % 2

    count_left, count_right = 2 * chip, 2 * (last - chip)
    lag_left, lag_right = 3 * (last - chip), 3 * chip

    activate(2 * chip)
    activate(2 * chip + 1)

    turns = max([2 * p + 3 * (last - p) for p in range(1, chips)])

    def turn(t, carry):
        for way, count in ((-1, count_left), (1, count_right)):

            @pl.when(t < count)
            def _():
                q = chunk_of(t, way)
                gather_copy(q, way).wait_recv()

                @pl.when(has_right if way == -1 else has_left)
                def _():
                    gather_copy(q, -way).start()

                activate(q)

        for way, count, lag in ((-1, count_left, lag_left), (1, count_right, lag_right)):
            n = t - lag

            @pl.when(jnp.logical_and(n >= 0, n < count))
            def _():
                q = chunk_of(n, way)
                slot = q if way == -1 else q + 2
                add_and_send(q, slot, way, has_right if way == -1 else has_left)

        return carry

    lax.fori_loop(0, turns, turn, 0)

    out_tile = rows // 5

    def rows_out(i, carry):
        part = pl.ds(pl.multiple_of(i * out_tile, out_tile), out_tile)

        def columns(k, inner):
            span = pl.ds(pl.multiple_of(k * piece, piece), piece)
            stage[0, :, span] = (
                jnp.dot(h_all[part, :], w_all[1, :, span], preferred_element_type=jnp.float32)
                * wt_ref[part, :]
            ).astype(jnp.bfloat16)
            stage[1, :, span] = jnp.dot(
                p_all[part, :], w_all[0, :, span], preferred_element_type=jnp.float32
            ).astype(jnp.bfloat16)
            return inner

        lax.fori_loop(0, 3, columns, 0)
        y_copy = pltpu.make_async_copy(stage.at[0], y_out.at[part], out_sem.at[0])
        gx_copy = pltpu.make_async_copy(stage.at[1], gx_out.at[part], out_sem.at[1])
        y_copy.start()
        gx_copy.start()
        y_copy.wait()
        gx_copy.wait()
        return carry

    lax.fori_loop(0, 5, rows_out, 0)

    def finish(sub, carry):
        q = 2 * chip + sub

        @pl.when(has_left)
        def _():
            sum_copy(q + 2, 1).wait_recv()

        @pl.when(has_right)
        def _():
            sum_copy(q, -1).wait_recv()

        @pl.when(jnp.logical_not(has_left))
        def _():
            sums[q + 2] = jnp.zeros(sums.shape[1:], sums.dtype)

        @pl.when(jnp.logical_not(has_right))
        def _():
            sums[q] = jnp.zeros(sums.shape[1:], sums.dtype)

        def emit(kind, span, value):
            dw_out[sub, kind, :, span] = (
                value
                + sums[q, kind, :, span].astype(jnp.float32)
                + sums[q + 2, kind, :, span].astype(jnp.float32)
            ).astype(jnp.bfloat16)

        weight_grads(q, emit)
        return carry

    lax.fori_loop(0, 2, finish, 0)

    for sub in range(2):

        @pl.when(has_left)
        def _():
            gather_copy(2 * chip + sub, -1).wait_send()

        @pl.when(has_right)
        def _():
            gather_copy(2 * chip + sub, 1).wait_send()

    def drain(n, carry):
        for way, count in ((-1, count_left), (1, count_right)):

            @pl.when(n < count)
            def _():
                q = chunk_of(n, way)

                @pl.when(has_right if way == -1 else has_left)
                def _():
                    gather_copy(q, -way).wait_send()

                sum_copy(q if way == -1 else q + 2, way).wait_send()

        return carry

    lax.fori_loop(0, 2 * last, drain, 0)


def run_experts(shards, x, g, weights, own_w):
    chips = shards // 2
    rows, width = x.shape
    depth = own_w.shape[1] // 2
    hidden = shards * depth
    slots = shards + 2
    vmem = pl.BlockSpec(memory_space=pltpu.VMEM)
    hbm = pl.BlockSpec(memory_space=pl.ANY)
    return pl.pallas_call(
        functools.partial(expert_kernel, chips),
        out_shape=(
            jax.ShapeDtypeStruct((rows, width), jnp.bfloat16),
            jax.ShapeDtypeStruct((rows, width), jnp.bfloat16),
            jax.ShapeDtypeStruct((2, 2, depth, width), jnp.bfloat16),
        ),
        in_specs=[vmem, vmem, vmem, hbm],
        out_specs=(hbm, hbm, vmem),
        scratch_shapes=[
            pltpu.VMEM((2, hidden, width), jnp.bfloat16),
            pltpu.VMEM((rows, hidden), jnp.bfloat16),
            pltpu.VMEM((rows, hidden), jnp.bfloat16),
            pltpu.VMEM((slots, 2, depth, width), jnp.bfloat16),
            pltpu.VMEM((2, rows // 5, width), jnp.bfloat16),
            pltpu.SemaphoreType.DMA((shards, 2)),
            pltpu.SemaphoreType.DMA((shards,)),
            pltpu.SemaphoreType.DMA((slots,)),
            pltpu.SemaphoreType.DMA((slots,)),
            pltpu.SemaphoreType.DMA,
            pltpu.SemaphoreType.DMA((2,)),
        ],
        compiler_params=pltpu.CompilerParams(
            collective_id=0, has_side_effects=True, vmem_limit_bytes=62 * 1024 * 1024
        ),
        cost_estimate=pl.CostEstimate(
            flops=12 * rows * width * hidden, bytes_accessed=30_000_000, transcendentals=0
        ),
    )(x, g, weights, own_w)


def body(shards, tokens, assign, gates, cot, w_in, w_out):
    own_count = w_in.shape[0]
    if own_count != 2:
        return plain_body(tokens, assign, gates, cot, w_in, w_out)
    block_count = assign.shape[0]
    block_len = tokens.shape[0] // block_count
    width = tokens.shape[1]
    rows = CAP * block_len
    core = lax.axis_index("dp") % 2
    pairs = [(i, i ^ 1) for i in range(shards)]

    def swap(array):
        return lax.ppermute(array, "dp", pairs)

    def mine(array):
        return lax.dynamic_index_in_dim(array, core, 0, keepdims=False)

    def other(array):
        return lax.dynamic_index_in_dim(array, 1 - core, 0, keepdims=False)

    both = jnp.stack([jnp.transpose(w_in, (0, 2, 1)), w_out], axis=1)
    kept, got = mine(both), swap(other(both))
    own_w = jnp.where(
        core == 0,
        jnp.concatenate([kept, got], axis=1),
        jnp.concatenate([got, kept], axis=1),
    )
    expert_ids = lax.axis_index("own") * own_count + jnp.arange(own_count, dtype=jnp.int32)
    blocks, is_valid, hits, ranks = jax.vmap(pick_blocks, (None, 0, None))(assign, expert_ids, CAP)
    gate_blocks = gates.reshape(block_count, block_len, 2)
    mixing = jax.vmap(block_gates, (None, None, 0, 0, 0))(
        assign, gate_blocks, blocks, is_valid, expert_ids
    )
    weight_rows = mixing.reshape(own_count, rows)
    token_blocks = tokens.reshape(block_count, block_len, width)
    picked = token_blocks[blocks].reshape(own_count, rows, width)
    cot_full = lax.all_gather(cot, "own", axis=1, tiled=True)
    cot_picked = cot_full.reshape(block_count, block_len, width)[blocks].reshape(
        own_count, rows, width
    )
    grad_out = (weight_rows[..., None] * cot_picked.astype(jnp.float32)).astype(jnp.bfloat16)

    def shared(array):
        return jnp.concatenate([mine(array), swap(other(array))], axis=0)

    x = shared(picked)
    g = shared(grad_out)
    weights = shared(weight_rows)[:, None]
    y, gx, dw = run_experts(shards, x, g, weights, own_w)

    my_hit, my_rank = mine(hits), mine(ranks)
    other_hit, other_rank = other(hits), other(ranks)

    def by_block(array):
        def take(part, hit, rank):
            chosen = part.reshape(CAP, block_len, width)[jnp.clip(rank, 0, CAP - 1)]
            return jnp.where(hit[:, None, None] == 1, chosen.astype(jnp.float32), 0.0)

        back = swap(array[rows:])
        total = take(array[:rows], my_hit, my_rank) + take(back, other_hit, other_rank)
        total = total.astype(jnp.bfloat16).reshape(block_count * block_len, width)
        return lax.psum_scatter(total, "own", scatter_dimension=1, tiled=True)

    mixed = by_block(y)
    grad_tokens = by_block(gx)
    dw_kept, dw_got = mine(dw), swap(other(dw))
    dw_all = jnp.where(
        core == 0, jnp.stack([dw_kept, dw_got]), jnp.stack([dw_got, dw_kept])
    ).astype(jnp.float32)
    grad_w_in = jnp.transpose(dw_all[:, 0], (0, 2, 1))
    return (mixed, grad_tokens, grad_w_in, dw_all[:, 1])


def gelu_cdf(values):
    return 0.5 * (1.0 + jax.scipy.special.erf(values * 0.7071067811865476))


def gelu_slope(values):
    return gelu_cdf(values) + values * jnp.exp(-0.5 * values * values) * 0.3989422804014327


def place_rows(terms, blocks, block_count):
    block_len = terms.shape[-2]
    width = terms.shape[-1]
    zeros = jnp.zeros((block_count, block_len, width), jnp.float32)
    placed = zeros.at[blocks.reshape(-1)].add(terms.reshape(-1, block_len, width))
    return placed.reshape(block_count * block_len, width)


def plain_body(tokens, assign, gates, cot, w_in, w_out):
    own_count = w_in.shape[0]
    block_count = assign.shape[0]
    block_len = tokens.shape[0] // block_count
    width = tokens.shape[1]
    full_in, full_out = (
        lax.all_gather(w_in, "dp", axis=2, tiled=True),
        lax.all_gather(w_out, "dp", axis=1, tiled=True),
    )
    expert_ids = lax.axis_index("own") * own_count + jnp.arange(own_count, dtype=jnp.int32)
    blocks, is_valid = jax.vmap(pick_blocks, (None, 0, None))(assign, expert_ids, CAP)[:2]
    gate_blocks = gates.reshape(block_count, block_len, 2)
    mixing = jax.vmap(block_gates, (None, None, 0, 0, 0))(
        assign, gate_blocks, blocks, is_valid, expert_ids
    )
    weight_rows = mixing.reshape(own_count, CAP * block_len)
    token_blocks = tokens.reshape(block_count, block_len, width)
    picked = token_blocks[blocks].reshape(own_count, CAP * block_len, width)
    pre_act = jnp.einsum("erd,edf->erf", picked, full_in, preferred_element_type=jnp.float32)
    hidden = (pre_act * gelu_cdf(pre_act)).astype(jnp.bfloat16)
    expert_out = jnp.einsum("erf,efd->erd", hidden, full_out, preferred_element_type=jnp.float32)
    contrib = (weight_rows[..., None] * expert_out).reshape(own_count, CAP, block_len, width)
    partial_rows = place_rows(contrib, blocks, block_count)
    mixed = lax.psum_scatter(
        partial_rows.astype(jnp.bfloat16), "own", scatter_dimension=1, tiled=True
    )
    cot_full = lax.all_gather(cot, "own", axis=1, tiled=True)
    cot_picked = cot_full.reshape(block_count, block_len, width)[blocks].reshape(
        own_count, CAP * block_len, width
    )
    grad_out = (weight_rows[..., None] * cot_picked.astype(jnp.float32)).astype(jnp.bfloat16)
    grad_hidden = jnp.einsum("erd,efd->erf", grad_out, full_out, preferred_element_type=jnp.float32)
    grad_pre = (grad_hidden * gelu_slope(pre_act)).astype(jnp.bfloat16)
    grad_in_terms = jnp.einsum(
        "erf,edf->erd", grad_pre, full_in, preferred_element_type=jnp.float32
    )
    grad_rows = place_rows(
        grad_in_terms.reshape(own_count, CAP, block_len, width), blocks, block_count
    )
    grad_tokens = lax.psum_scatter(
        grad_rows.astype(jnp.bfloat16), "own", scatter_dimension=1, tiled=True
    )
    out_full = jnp.einsum("erf,erd->efd", hidden, grad_out, preferred_element_type=jnp.float32)
    in_full = jnp.einsum("erf,erd->efd", grad_pre, picked, preferred_element_type=jnp.float32)
    grad_w_out, in_shard = (
        lax.psum_scatter(
            out_full.astype(jnp.bfloat16), "dp", scatter_dimension=1, tiled=True
        ).astype(jnp.float32),
        lax.psum_scatter(
            in_full.astype(jnp.bfloat16), "dp", scatter_dimension=1, tiled=True
        ).astype(jnp.float32),
    )
    grad_w_in = jnp.transpose(in_shard, (0, 2, 1))
    return (mixed, grad_tokens, grad_w_in, grad_w_out)


def solution(mesh):
    placed = (
        P("dp", None),
        P("dp", None),
        P("dp", None),
        P("dp", "own"),
        P("own", None, "dp"),
        P("own", "dp", None),
    )
    return jax.shard_map(
        functools.partial(body, mesh.shape["dp"]),
        mesh=mesh,
        in_specs=placed,
        out_specs=(P("dp", "own"), P("dp", "own"), P("own", None, "dp"), P("own", "dp", None)),
        check_vma=False,
    )
```

```python
import functools

import jax
import jax.numpy as jnp
from jax import lax
from jax.experimental import pallas as pl
from jax.experimental.pallas import tpu as pltpu
from jax.sharding import PartitionSpec as P

CAP = 5
MESH = pl.DeviceIdType.MESH


def pick_blocks(assign_rows, expert, capacity):
    hit_flag = jnp.logical_or(assign_rows[:, 0] == expert, assign_rows[:, 1] == expert).astype(
        jnp.int32
    )
    slot_rank = jnp.cumsum(hit_flag) - 1
    slot_ids = jnp.arange(capacity, dtype=jnp.int32)
    matches = jnp.logical_and(
        hit_flag[None, :] == 1, slot_rank[None, :] == slot_ids[:, None]
    ).astype(jnp.int32)
    where_idx = jnp.arange(assign_rows.shape[0], dtype=jnp.int32)
    blocks = jnp.sum(matches * where_idx[None, :], axis=1)
    is_valid = jnp.sum(matches, axis=1).astype(jnp.float32)
    return (blocks, is_valid, hit_flag, slot_rank)


def block_gates(assign_rows, gate_blocks, blocks, is_valid, expert):
    chosen = assign_rows[blocks]
    picked_gates = gate_blocks[blocks]
    first_hit = (chosen[:, 0] == expert).astype(jnp.float32)
    second_hit = (chosen[:, 1] == expert).astype(jnp.float32)
    mixing = picked_gates[..., 0] * first_hit[:, None] + picked_gates[..., 1] * second_hit[:, None]
    return mixing * is_valid[:, None]


def expert_kernel(
    chips,
    x_mine,
    x_theirs,
    g_mine,
    g_theirs,
    wt_ref,
    w_mine,
    w_theirs,
    y_mine,
    y_theirs,
    gx_mine,
    gx_theirs,
    dw_mine,
    dw_theirs,
    x_ref,
    g_ref,
    w_all,
    h_all,
    p_all,
    sums,
    stage,
    ag_send,
    ag_recv,
    rs_send,
    rs_recv,
    own_sem,
    in_sem,
    out_sem,
):
    me = lax.axis_index("dp")
    chip, core = me // 2, me % 2
    rows, width = x_ref.shape
    half = rows // 2
    depth = w_mine.shape[1]
    last = chips - 1
    has_left, has_right = chip > 0, chip < last

    def at_chunk(ref, q):
        return ref.at[:, pl.ds(pl.multiple_of(q * depth, depth), depth)]

    def gather_copy(q, way):
        return pltpu.make_async_remote_copy(
            src_ref=at_chunk(w_all, q),
            dst_ref=at_chunk(w_all, q),
            send_sem=ag_send.at[q, (way + 1) // 2],
            recv_sem=ag_recv.at[q],
            device_id={"dp": me + 2 * way},
            device_id_type=MESH,
        )

    def sum_copy(slot, way):
        return pltpu.make_async_remote_copy(
            src_ref=sums.at[slot],
            dst_ref=sums.at[slot],
            send_sem=rs_send.at[slot],
            recv_sem=rs_recv.at[slot],
            device_id={"dp": me + 2 * way},
            device_id_type=MESH,
        )

    own_copies = [
        pltpu.make_async_copy(src, at_chunk(w_all, 2 * chip + place), own_sem.at[i])
        for i, (src, place) in enumerate(((w_mine, core), (w_theirs, 1 - core)))
    ]
    for copy in own_copies:
        copy.start()
    in_copies = [
        pltpu.make_async_copy(src, dst, in_sem.at[i])
        for i, (src, dst) in enumerate(
            (
                (x_mine, x_ref.at[:half]),
                (x_theirs, x_ref.at[half:]),
                (g_mine, g_ref.at[:half]),
                (g_theirs, g_ref.at[half:]),
            )
        )
    ]
    for copy in in_copies:
        copy.start()
    barrier = pltpu.get_barrier_semaphore()

    @pl.when(has_left)
    def _():
        pl.semaphore_signal(barrier, inc=1, device_id={"dp": me - 2}, device_id_type=MESH)

    @pl.when(has_right)
    def _():
        pl.semaphore_signal(barrier, inc=1, device_id={"dp": me + 2}, device_id_type=MESH)

    pl.semaphore_wait(barrier, has_left.astype(jnp.int32) + has_right.astype(jnp.int32))

    for copy in own_copies:
        copy.wait()
    for sub in range(2):

        @pl.when(has_left)
        def _():
            gather_copy(2 * chip + sub, -1).start()

        @pl.when(has_right)
        def _():
            gather_copy(2 * chip + sub, 1).start()

    for copy in in_copies:
        copy.wait()

    tile = half
    nt = (((1,), (1,)), ((), ()))

    def activate(q):
        cols = pl.ds(pl.multiple_of(q * depth, depth), depth)

        def step(r, carry):
            part = pl.ds(pl.multiple_of(r * tile, tile), tile)
            pre = lax.dot_general(
                x_ref[part, :], w_all[0, cols, :], nt, preferred_element_type=jnp.float32
            )
            grad_hidden = lax.dot_general(
                g_ref[part, :], w_all[1, cols, :], nt, preferred_element_type=jnp.float32
            )
            cdf = 0.5 * (1.0 + lax.erf(pre * 0.7071067811865476))
            slope = cdf + pre * jnp.exp(-0.5 * pre * pre) * 0.3989422804014327
            h_all[part, cols] = (pre * cdf).astype(jnp.bfloat16)
            p_all[part, cols] = (grad_hidden * slope).astype(jnp.bfloat16)
            return carry

        lax.fori_loop(0, 2, step, 0)

    piece = width // 3

    def weight_grads(q, emit):
        cols = pl.ds(pl.multiple_of(q * depth, depth), depth)
        for kind, left, right in ((0, p_all, x_ref), (1, h_all, g_ref)):
            turned = left[:, cols].T

            def step(k, carry):
                span = pl.ds(pl.multiple_of(k * piece, piece), piece)
                emit(
                    kind,
                    span,
                    jnp.dot(turned, right[:, span], preferred_element_type=jnp.float32),
                )
                return carry

            lax.fori_loop(0, 3, step, 0)

    def add_and_send(q, slot, way, fed):
        @pl.when(fed)
        def _():
            sum_copy(slot, way).wait_recv()

        @pl.when(jnp.logical_not(fed))
        def _():
            sums[slot] = jnp.zeros(sums.shape[1:], sums.dtype)

        def emit(kind, span, value):
            sums[slot, kind, :, span] = (
                value + sums[slot, kind, :, span].astype(jnp.float32)
            ).astype(jnp.bfloat16)

        weight_grads(q, emit)
        sum_copy(slot, way).start()

    def chunk_of(n, way):
        return 2 * (chip + way * (1 + n // 2)) + n % 2

    count_left, count_right = 2 * chip, 2 * (last - chip)
    lag_left, lag_right = 3 * (last - chip), 3 * chip

    activate(2 * chip)
    activate(2 * chip + 1)

    turns = max([2 * p + 3 * (last - p) for p in range(1, chips)])

    def turn(t, carry):
        for way, count in ((-1, count_left), (1, count_right)):

            @pl.when(t < count)
            def _():
                q = chunk_of(t, way)
                gather_copy(q, way).wait_recv()

                @pl.when(has_right if way == -1 else has_left)
                def _():
                    gather_copy(q, -way).start()

                activate(q)

        for way, count, lag in ((-1, count_left, lag_left), (1, count_right, lag_right)):
            n = t - lag

            @pl.when(jnp.logical_and(n >= 0, n < count))
            def _():
                q = chunk_of(n, way)
                slot = q if way == -1 else q + 2
                add_and_send(q, slot, way, has_right if way == -1 else has_left)

        return carry

    lax.fori_loop(0, turns, turn, 0)

    blocks, columns, block_len, share = y_mine.shape

    for side, (y_out, gx_out) in enumerate(((y_mine, gx_mine), (y_theirs, gx_theirs))):
        part = pl.ds(side * half, half)

        def column(k, carry):
            span = pl.ds(pl.multiple_of(k * share, share), share)
            y = jnp.dot(h_all[part, :], w_all[1, :, span], preferred_element_type=jnp.float32)
            y = (y * wt_ref[part, :]).astype(jnp.bfloat16)
            gx = jnp.dot(p_all[part, :], w_all[0, :, span], preferred_element_type=jnp.float32)
            gx = gx.astype(jnp.bfloat16)
            for b in range(blocks):
                stage[0, b, k] = y[b * block_len : (b + 1) * block_len]
                stage[1, b, k] = gx[b * block_len : (b + 1) * block_len]
            return carry

        lax.fori_loop(0, columns, column, 0)
        y_copy = pltpu.make_async_copy(stage.at[0], y_out, out_sem.at[0])
        gx_copy = pltpu.make_async_copy(stage.at[1], gx_out, out_sem.at[1])
        y_copy.start()
        gx_copy.start()
        y_copy.wait()
        gx_copy.wait()

    def finish(q, dw_out):

        @pl.when(has_left)
        def _():
            sum_copy(q + 2, 1).wait_recv()

        @pl.when(has_right)
        def _():
            sum_copy(q, -1).wait_recv()

        @pl.when(jnp.logical_not(has_left))
        def _():
            sums[q + 2] = jnp.zeros(sums.shape[1:], sums.dtype)

        @pl.when(jnp.logical_not(has_right))
        def _():
            sums[q] = jnp.zeros(sums.shape[1:], sums.dtype)

        def emit(kind, span, value):
            dw_out[kind, :, span] = (
                value
                + sums[q, kind, :, span].astype(jnp.float32)
                + sums[q + 2, kind, :, span].astype(jnp.float32)
            ).astype(jnp.bfloat16)

        weight_grads(q, emit)

    finish(2 * chip + 1 - core, dw_theirs)
    finish(2 * chip + core, dw_mine)

    for sub in range(2):

        @pl.when(has_left)
        def _():
            gather_copy(2 * chip + sub, -1).wait_send()

        @pl.when(has_right)
        def _():
            gather_copy(2 * chip + sub, 1).wait_send()

    def drain(n, carry):
        for way, count in ((-1, count_left), (1, count_right)):

            @pl.when(n < count)
            def _():
                q = chunk_of(n, way)

                @pl.when(has_right if way == -1 else has_left)
                def _():
                    gather_copy(q, -way).wait_send()

                sum_copy(q if way == -1 else q + 2, way).wait_send()

        return carry

    lax.fori_loop(0, 2 * last, drain, 0)


def run_experts(shards, owners, x, g, weights, own_w):
    chips = shards // 2
    half, width = x[0].shape
    rows = 2 * half
    depth = own_w[0].shape[1]
    hidden = shards * depth
    slots = shards + 2
    vmem = pl.BlockSpec(memory_space=pltpu.VMEM)
    hbm = pl.BlockSpec(memory_space=pl.ANY)
    token_out = jax.ShapeDtypeStruct((CAP, owners, half // CAP, width // owners), jnp.bfloat16)
    weight_out = jax.ShapeDtypeStruct((2, depth, width), jnp.bfloat16)
    return pl.pallas_call(
        functools.partial(expert_kernel, chips),
        out_shape=(token_out,) * 4 + (weight_out,) * 2,
        in_specs=[hbm] * 4 + [vmem] + [hbm] * 2,
        out_specs=(hbm,) * 4 + (vmem,) * 2,
        scratch_shapes=[
            pltpu.VMEM((rows, width), jnp.bfloat16),
            pltpu.VMEM((rows, width), jnp.bfloat16),
            pltpu.VMEM((2, hidden, width), jnp.bfloat16),
            pltpu.VMEM((rows, hidden), jnp.bfloat16),
            pltpu.VMEM((rows, hidden), jnp.bfloat16),
            pltpu.VMEM((slots, 2, depth, width), jnp.bfloat16),
            pltpu.VMEM((2,) + token_out.shape, jnp.bfloat16),
            pltpu.SemaphoreType.DMA((shards, 2)),
            pltpu.SemaphoreType.DMA((shards,)),
            pltpu.SemaphoreType.DMA((slots,)),
            pltpu.SemaphoreType.DMA((slots,)),
            pltpu.SemaphoreType.DMA((2,)),
            pltpu.SemaphoreType.DMA((4,)),
            pltpu.SemaphoreType.DMA((2,)),
        ],
        compiler_params=pltpu.CompilerParams(
            collective_id=0, has_side_effects=True, vmem_limit_bytes=62 * 1024 * 1024
        ),
        cost_estimate=pl.CostEstimate(
            flops=12 * rows * width * hidden, bytes_accessed=30_000_000, transcendentals=0
        ),
    )(*x, *g, weights, *own_w)


def body(shards, owners, tokens, assign, gates, cot, w_in, w_out):
    own_count = w_in.shape[0]
    if own_count != 2:
        return plain_body(tokens, assign, gates, cot, w_in, w_out)
    block_count = assign.shape[0]
    block_len = tokens.shape[0] // block_count
    width = tokens.shape[1]
    rows = CAP * block_len
    core = lax.axis_index("dp") % 2
    pairs = [(i, i ^ 1) for i in range(shards)]

    def swap(array):
        return lax.ppermute(array, "dp", pairs)

    def mine(array):
        return lax.dynamic_index_in_dim(array, core, 0, keepdims=False)

    def other(array):
        return lax.dynamic_index_in_dim(array, 1 - core, 0, keepdims=False)

    both = jnp.stack([jnp.transpose(w_in, (0, 2, 1)), w_out], axis=1)
    own_w = (mine(both), swap(other(both)))
    expert_ids = lax.axis_index("own") * own_count + jnp.arange(own_count, dtype=jnp.int32)
    blocks, is_valid, hits, ranks = jax.vmap(pick_blocks, (None, 0, None))(assign, expert_ids, CAP)
    gate_blocks = gates.reshape(block_count, block_len, 2)
    mixing = jax.vmap(block_gates, (None, None, 0, 0, 0))(
        assign, gate_blocks, blocks, is_valid, expert_ids
    )
    weight_rows = mixing.reshape(own_count, rows)
    token_blocks = tokens.reshape(block_count, block_len, width)
    picked = token_blocks[blocks].reshape(own_count, rows, width)
    cot_full = lax.all_gather(cot, "own", axis=1, tiled=True)
    cot_picked = cot_full.reshape(block_count, block_len, width)[blocks].reshape(
        own_count, rows, width
    )
    grad_out = (weight_rows[..., None] * cot_picked.astype(jnp.float32)).astype(jnp.bfloat16)

    def shared(array):
        return (mine(array), swap(other(array)))

    x = shared(picked)
    g = shared(grad_out)
    weights = jnp.concatenate(shared(weight_rows))[:, None]
    y_mine, y_theirs, gx_mine, gx_theirs, dw_mine, dw_theirs = run_experts(
        shards, owners, x, g, weights, own_w
    )

    my_hit, my_rank = mine(hits), mine(ranks)
    other_hit, other_rank = other(hits), other(ranks)

    def by_block(kept, back):
        def take(part, hit, rank):
            chosen = part[jnp.clip(rank, 0, CAP - 1)]
            return jnp.where(hit[:, None, None, None] == 1, chosen.astype(jnp.float32), 0.0)

        total = take(kept, my_hit, my_rank) + take(back, other_hit, other_rank)
        total = jnp.swapaxes(total.astype(jnp.bfloat16), 0, 1)
        return total.reshape(owners, block_count * block_len, width // owners)

    y_back, gx_back, dw_got = swap(y_theirs), swap(gx_theirs), swap(dw_theirs)
    y_total = by_block(y_mine, y_back)
    y_total, gx_mine, gx_back = lax.optimization_barrier((y_total, gx_mine, gx_back))
    mixed = lax.psum_scatter(y_total, "own", scatter_dimension=0, tiled=False)
    grad_tokens = lax.psum_scatter(
        by_block(gx_mine, gx_back), "own", scatter_dimension=0, tiled=False
    )
    dw_kept = dw_mine
    dw_all = jnp.where(
        core == 0, jnp.stack([dw_kept, dw_got]), jnp.stack([dw_got, dw_kept])
    ).astype(jnp.float32)
    grad_w_in = jnp.transpose(dw_all[:, 0], (0, 2, 1))
    return (mixed, grad_tokens, grad_w_in, dw_all[:, 1])


def gelu_cdf(values):
    return 0.5 * (1.0 + jax.scipy.special.erf(values * 0.7071067811865476))


def gelu_slope(values):
    return gelu_cdf(values) + values * jnp.exp(-0.5 * values * values) * 0.3989422804014327


def place_rows(terms, blocks, block_count):
    block_len = terms.shape[-2]
    width = terms.shape[-1]
    zeros = jnp.zeros((block_count, block_len, width), jnp.float32)
    placed = zeros.at[blocks.reshape(-1)].add(terms.reshape(-1, block_len, width))
    return placed.reshape(block_count * block_len, width)


def plain_body(tokens, assign, gates, cot, w_in, w_out):
    own_count = w_in.shape[0]
    block_count = assign.shape[0]
    block_len = tokens.shape[0] // block_count
    width = tokens.shape[1]
    full_in, full_out = (
        lax.all_gather(w_in, "dp", axis=2, tiled=True),
        lax.all_gather(w_out, "dp", axis=1, tiled=True),
    )
    expert_ids = lax.axis_index("own") * own_count + jnp.arange(own_count, dtype=jnp.int32)
    blocks, is_valid = jax.vmap(pick_blocks, (None, 0, None))(assign, expert_ids, CAP)[:2]
    gate_blocks = gates.reshape(block_count, block_len, 2)
    mixing = jax.vmap(block_gates, (None, None, 0, 0, 0))(
        assign, gate_blocks, blocks, is_valid, expert_ids
    )
    weight_rows = mixing.reshape(own_count, CAP * block_len)
    token_blocks = tokens.reshape(block_count, block_len, width)
    picked = token_blocks[blocks].reshape(own_count, CAP * block_len, width)
    pre_act = jnp.einsum("erd,edf->erf", picked, full_in, preferred_element_type=jnp.float32)
    hidden = (pre_act * gelu_cdf(pre_act)).astype(jnp.bfloat16)
    expert_out = jnp.einsum("erf,efd->erd", hidden, full_out, preferred_element_type=jnp.float32)
    contrib = (weight_rows[..., None] * expert_out).reshape(own_count, CAP, block_len, width)
    partial_rows = place_rows(contrib, blocks, block_count)
    mixed = lax.psum_scatter(
        partial_rows.astype(jnp.bfloat16), "own", scatter_dimension=1, tiled=True
    )
    cot_full = lax.all_gather(cot, "own", axis=1, tiled=True)
    cot_picked = cot_full.reshape(block_count, block_len, width)[blocks].reshape(
        own_count, CAP * block_len, width
    )
    grad_out = (weight_rows[..., None] * cot_picked.astype(jnp.float32)).astype(jnp.bfloat16)
    grad_hidden = jnp.einsum("erd,efd->erf", grad_out, full_out, preferred_element_type=jnp.float32)
    grad_pre = (grad_hidden * gelu_slope(pre_act)).astype(jnp.bfloat16)
    grad_in_terms = jnp.einsum(
        "erf,edf->erd", grad_pre, full_in, preferred_element_type=jnp.float32
    )
    grad_rows = place_rows(
        grad_in_terms.reshape(own_count, CAP, block_len, width), blocks, block_count
    )
    grad_tokens = lax.psum_scatter(
        grad_rows.astype(jnp.bfloat16), "own", scatter_dimension=1, tiled=True
    )
    out_full = jnp.einsum("erf,erd->efd", hidden, grad_out, preferred_element_type=jnp.float32)
    in_full = jnp.einsum("erf,erd->efd", grad_pre, picked, preferred_element_type=jnp.float32)
    grad_w_out, in_shard = (
        lax.psum_scatter(
            out_full.astype(jnp.bfloat16), "dp", scatter_dimension=1, tiled=True
        ).astype(jnp.float32),
        lax.psum_scatter(
            in_full.astype(jnp.bfloat16), "dp", scatter_dimension=1, tiled=True
        ).astype(jnp.float32),
    )
    grad_w_in = jnp.transpose(in_shard, (0, 2, 1))
    return (mixed, grad_tokens, grad_w_in, grad_w_out)


def solution(mesh):
    placed = (
        P("dp", None),
        P("dp", None),
        P("dp", None),
        P("dp", "own"),
        P("own", None, "dp"),
        P("own", "dp", None),
    )
    return jax.shard_map(
        functools.partial(body, mesh.shape["dp"], mesh.shape["own"]),
        mesh=mesh,
        in_specs=placed,
        out_specs=(P("dp", "own"), P("dp", "own"), P("own", None, "dp"), P("own", "dp", None)),
        check_vma=False,
    )
```

```python
import functools

import jax
import jax.numpy as jnp
from jax import lax
from jax.experimental import pallas as pl
from jax.experimental.pallas import tpu as pltpu
from jax.sharding import PartitionSpec as P

CAP = 5
MESH = pl.DeviceIdType.MESH


def pick_blocks(assign_rows, expert, capacity):
    hit_flag = jnp.logical_or(assign_rows[:, 0] == expert, assign_rows[:, 1] == expert).astype(
        jnp.int32
    )
    slot_rank = jnp.cumsum(hit_flag) - 1
    slot_ids = jnp.arange(capacity, dtype=jnp.int32)
    matches = jnp.logical_and(
        hit_flag[None, :] == 1, slot_rank[None, :] == slot_ids[:, None]
    ).astype(jnp.int32)
    where_idx = jnp.arange(assign_rows.shape[0], dtype=jnp.int32)
    blocks = jnp.sum(matches * where_idx[None, :], axis=1)
    is_valid = jnp.sum(matches, axis=1).astype(jnp.float32)
    return (blocks, is_valid, hit_flag, slot_rank)


def block_gates(assign_rows, gate_blocks, blocks, is_valid, expert):
    chosen = assign_rows[blocks]
    picked_gates = gate_blocks[blocks]
    first_hit = (chosen[:, 0] == expert).astype(jnp.float32)
    second_hit = (chosen[:, 1] == expert).astype(jnp.float32)
    mixing = picked_gates[..., 0] * first_hit[:, None] + picked_gates[..., 1] * second_hit[:, None]
    return mixing * is_valid[:, None]


def expert_kernel(
    chips,
    x_mine,
    x_theirs,
    g_mine,
    g_theirs,
    wt_ref,
    w_mine,
    w_theirs,
    y_mine,
    y_theirs,
    gx_mine,
    gx_theirs,
    dw_mine,
    dw_theirs,
    x_ref,
    g_ref,
    w_all,
    h_all,
    p_all,
    sums,
    stage,
    ag_send,
    ag_recv,
    rs_send,
    rs_recv,
    own_sem,
    in_sem,
    out_sem,
):
    me = lax.axis_index("dp")
    chip, core = me // 2, me % 2
    rows, width = x_ref.shape
    half = rows // 2
    depth = w_mine.shape[1]
    last = chips - 1
    has_left, has_right = chip > 0, chip < last

    def at_chunk(ref, q):
        return ref.at[:, pl.ds(pl.multiple_of(q * depth, depth), depth)]

    def gather_copy(q, way):
        return pltpu.make_async_remote_copy(
            src_ref=at_chunk(w_all, q),
            dst_ref=at_chunk(w_all, q),
            send_sem=ag_send.at[q, (way + 1) // 2],
            recv_sem=ag_recv.at[q],
            device_id={"dp": me + 2 * way},
            device_id_type=MESH,
        )

    def sum_copy(slot, way):
        return pltpu.make_async_remote_copy(
            src_ref=sums.at[slot],
            dst_ref=sums.at[slot],
            send_sem=rs_send.at[slot],
            recv_sem=rs_recv.at[slot],
            device_id={"dp": me + 2 * way},
            device_id_type=MESH,
        )

    own_copies = [
        pltpu.make_async_copy(src, at_chunk(w_all, 2 * chip + place), own_sem.at[i])
        for i, (src, place) in enumerate(((w_mine, core), (w_theirs, 1 - core)))
    ]
    for copy in own_copies:
        copy.start()
    in_copies = [
        pltpu.make_async_copy(src, dst, in_sem.at[i])
        for i, (src, dst) in enumerate(
            (
                (x_mine, x_ref.at[:half]),
                (x_theirs, x_ref.at[half:]),
                (g_mine, g_ref.at[:half]),
                (g_theirs, g_ref.at[half:]),
            )
        )
    ]
    for copy in in_copies:
        copy.start()
    barrier = pltpu.get_barrier_semaphore()

    @pl.when(has_left)
    def _():
        pl.semaphore_signal(barrier, inc=1, device_id={"dp": me - 2}, device_id_type=MESH)

    @pl.when(has_right)
    def _():
        pl.semaphore_signal(barrier, inc=1, device_id={"dp": me + 2}, device_id_type=MESH)

    pl.semaphore_wait(barrier, has_left.astype(jnp.int32) + has_right.astype(jnp.int32))

    for copy in own_copies:
        copy.wait()
    for sub in range(2):

        @pl.when(has_left)
        def _():
            gather_copy(2 * chip + sub, -1).start()

        @pl.when(has_right)
        def _():
            gather_copy(2 * chip + sub, 1).start()

    for copy in in_copies:
        copy.wait()

    tile = half
    nt = (((1,), (1,)), ((), ()))

    def activate(q):
        cols = pl.ds(pl.multiple_of(q * depth, depth), depth)

        def step(r, carry):
            part = pl.ds(pl.multiple_of(r * tile, tile), tile)
            pre = lax.dot_general(
                x_ref[part, :], w_all[0, cols, :], nt, preferred_element_type=jnp.float32
            )
            grad_hidden = lax.dot_general(
                g_ref[part, :], w_all[1, cols, :], nt, preferred_element_type=jnp.float32
            )
            cdf = 0.5 * (1.0 + lax.erf(pre * 0.7071067811865476))
            slope = cdf + pre * jnp.exp(-0.5 * pre * pre) * 0.3989422804014327
            h_all[part, cols] = (pre * cdf).astype(jnp.bfloat16)
            p_all[part, cols] = (grad_hidden * slope).astype(jnp.bfloat16)
            return carry

        lax.fori_loop(0, 2, step, 0)

    piece = width // 3

    def weight_grads(q, emit):
        cols = pl.ds(pl.multiple_of(q * depth, depth), depth)
        for kind, left, right in ((0, p_all, x_ref), (1, h_all, g_ref)):
            turned = left[:, cols].T

            def step(k, carry):
                span = pl.ds(pl.multiple_of(k * piece, piece), piece)
                emit(
                    kind,
                    span,
                    jnp.dot(turned, right[:, span], preferred_element_type=jnp.float32),
                )
                return carry

            lax.fori_loop(0, 3, step, 0)

    def add_and_send(q, slot, way, fed):
        @pl.when(fed)
        def _():
            sum_copy(slot, way).wait_recv()

        @pl.when(jnp.logical_not(fed))
        def _():
            sums[slot] = jnp.zeros(sums.shape[1:], sums.dtype)

        def emit(kind, span, value):
            sums[slot, kind, :, span] = (
                value + sums[slot, kind, :, span].astype(jnp.float32)
            ).astype(jnp.bfloat16)

        weight_grads(q, emit)
        sum_copy(slot, way).start()

    def chunk_of(n, way):
        return 2 * (chip + way * (1 + n // 2)) + n % 2

    count_left, count_right = 2 * chip, 2 * (last - chip)
    lag_left, lag_right = 3 * (last - chip), 3 * chip

    activate(2 * chip)
    activate(2 * chip + 1)

    turns = max([2 * p + 3 * (last - p) for p in range(1, chips)])

    def turn(t, carry):
        for way, count in ((-1, count_left), (1, count_right)):

            @pl.when(t < count)
            def _():
                q = chunk_of(t, way)
                gather_copy(q, way).wait_recv()

                @pl.when(has_right if way == -1 else has_left)
                def _():
                    gather_copy(q, -way).start()

                activate(q)

        for way, count, lag in ((-1, count_left, lag_left), (1, count_right, lag_right)):
            n = t - lag

            @pl.when(jnp.logical_and(n >= 0, n < count))
            def _():
                q = chunk_of(n, way)
                slot = q if way == -1 else q + 2
                add_and_send(q, slot, way, has_right if way == -1 else has_left)

        return carry

    lax.fori_loop(0, turns, turn, 0)

    blocks, columns, block_len, share = y_mine.shape

    for side, (y_out, gx_out) in enumerate(((y_mine, gx_mine), (y_theirs, gx_theirs))):
        part = pl.ds(side * half, half)

        def column(k, carry):
            span = pl.ds(pl.multiple_of(k * share, share), share)
            y = jnp.dot(h_all[part, :], w_all[1, :, span], preferred_element_type=jnp.float32)
            y = (y * wt_ref[part, :]).astype(jnp.bfloat16)
            gx = jnp.dot(p_all[part, :], w_all[0, :, span], preferred_element_type=jnp.float32)
            gx = gx.astype(jnp.bfloat16)
            for b in range(blocks):
                stage[0, b, k] = y[b * block_len : (b + 1) * block_len]
                stage[1, b, k] = gx[b * block_len : (b + 1) * block_len]
            return carry

        lax.fori_loop(0, columns, column, 0)
        y_copy = pltpu.make_async_copy(stage.at[0], y_out, out_sem.at[0])
        gx_copy = pltpu.make_async_copy(stage.at[1], gx_out, out_sem.at[1])
        y_copy.start()
        gx_copy.start()
        y_copy.wait()
        gx_copy.wait()

    def finish(q, dw_out):

        @pl.when(has_left)
        def _():
            sum_copy(q + 2, 1).wait_recv()

        @pl.when(has_right)
        def _():
            sum_copy(q, -1).wait_recv()

        @pl.when(jnp.logical_not(has_left))
        def _():
            sums[q + 2] = jnp.zeros(sums.shape[1:], sums.dtype)

        @pl.when(jnp.logical_not(has_right))
        def _():
            sums[q] = jnp.zeros(sums.shape[1:], sums.dtype)

        def emit(kind, span, value):
            dw_out[kind, :, span] = (
                value
                + sums[q, kind, :, span].astype(jnp.float32)
                + sums[q + 2, kind, :, span].astype(jnp.float32)
            ).astype(jnp.bfloat16)

        weight_grads(q, emit)

    finish(2 * chip + 1 - core, dw_theirs)
    finish(2 * chip + core, dw_mine)

    for sub in range(2):

        @pl.when(has_left)
        def _():
            gather_copy(2 * chip + sub, -1).wait_send()

        @pl.when(has_right)
        def _():
            gather_copy(2 * chip + sub, 1).wait_send()

    def drain(n, carry):
        for way, count in ((-1, count_left), (1, count_right)):

            @pl.when(n < count)
            def _():
                q = chunk_of(n, way)

                @pl.when(has_right if way == -1 else has_left)
                def _():
                    gather_copy(q, -way).wait_send()

                sum_copy(q if way == -1 else q + 2, way).wait_send()

        return carry

    lax.fori_loop(0, 2 * last, drain, 0)


def run_experts(shards, owners, x, g, weights, own_w):
    chips = shards // 2
    half, width = x[0].shape
    rows = 2 * half
    depth = own_w[0].shape[1]
    hidden = shards * depth
    slots = shards + 2
    vmem = pl.BlockSpec(memory_space=pltpu.VMEM)
    hbm = pl.BlockSpec(memory_space=pl.ANY)
    token_out = jax.ShapeDtypeStruct((CAP, owners, half // CAP, width // owners), jnp.bfloat16)
    weight_out = jax.ShapeDtypeStruct((2, depth, width), jnp.bfloat16)
    return pl.pallas_call(
        functools.partial(expert_kernel, chips),
        out_shape=(token_out,) * 4 + (weight_out,) * 2,
        in_specs=[hbm] * 4 + [vmem] + [hbm] * 2,
        out_specs=(hbm,) * 4 + (vmem,) * 2,
        scratch_shapes=[
            pltpu.VMEM((rows, width), jnp.bfloat16),
            pltpu.VMEM((rows, width), jnp.bfloat16),
            pltpu.VMEM((2, hidden, width), jnp.bfloat16),
            pltpu.VMEM((rows, hidden), jnp.bfloat16),
            pltpu.VMEM((rows, hidden), jnp.bfloat16),
            pltpu.VMEM((slots, 2, depth, width), jnp.bfloat16),
            pltpu.VMEM((2,) + token_out.shape, jnp.bfloat16),
            pltpu.SemaphoreType.DMA((shards, 2)),
            pltpu.SemaphoreType.DMA((shards,)),
            pltpu.SemaphoreType.DMA((slots,)),
            pltpu.SemaphoreType.DMA((slots,)),
            pltpu.SemaphoreType.DMA((2,)),
            pltpu.SemaphoreType.DMA((4,)),
            pltpu.SemaphoreType.DMA((2,)),
        ],
        compiler_params=pltpu.CompilerParams(
            collective_id=0, has_side_effects=True, vmem_limit_bytes=62 * 1024 * 1024
        ),
        cost_estimate=pl.CostEstimate(
            flops=12 * rows * width * hidden, bytes_accessed=30_000_000, transcendentals=0
        ),
    )(*x, *g, weights, *own_w)


def body(shards, owners, tokens, assign, gates, cot, w_in, w_out):
    own_count = w_in.shape[0]
    if own_count != 2:
        return plain_body(tokens, assign, gates, cot, w_in, w_out)
    block_count = assign.shape[0]
    block_len = tokens.shape[0] // block_count
    width = tokens.shape[1]
    rows = CAP * block_len
    core = lax.axis_index("dp") % 2
    pairs = [(i, i ^ 1) for i in range(shards)]

    def swap(array):
        return lax.ppermute(array, "dp", pairs)

    owner = lax.axis_index("own")

    def exchange(array, step):
        return lax.ppermute(array, "own", [(i, i ^ step) for i in range(owners)])

    def mine(array):
        return lax.dynamic_index_in_dim(array, core, 0, keepdims=False)

    def other(array):
        return lax.dynamic_index_in_dim(array, 1 - core, 0, keepdims=False)

    both = jnp.stack([jnp.transpose(w_in, (0, 2, 1)), w_out], axis=1)
    own_w = (mine(both), swap(other(both)))
    expert_ids = lax.axis_index("own") * own_count + jnp.arange(own_count, dtype=jnp.int32)
    blocks, is_valid, hits, ranks = jax.vmap(pick_blocks, (None, 0, None))(assign, expert_ids, CAP)
    gate_blocks = gates.reshape(block_count, block_len, 2)
    mixing = jax.vmap(block_gates, (None, None, 0, 0, 0))(
        assign, gate_blocks, blocks, is_valid, expert_ids
    )
    weight_rows = mixing.reshape(own_count, rows)
    token_blocks = tokens.reshape(block_count, block_len, width)
    picked = token_blocks[blocks].reshape(own_count, rows, width)
    cot_full = jnp.zeros((cot.shape[0], width), cot.dtype)
    for step in range(owners):
        part = exchange(cot, step) if step else cot
        cot_full = lax.dynamic_update_slice_in_dim(
            cot_full, part, (owner ^ step) * cot.shape[1], axis=1
        )
    cot_picked = cot_full.reshape(block_count, block_len, width)[blocks].reshape(
        own_count, rows, width
    )
    grad_out = (weight_rows[..., None] * cot_picked.astype(jnp.float32)).astype(jnp.bfloat16)

    def shared(array):
        return (mine(array), swap(other(array)))

    x = shared(picked)
    g = shared(grad_out)
    weights = jnp.concatenate(shared(weight_rows))[:, None]
    y_mine, y_theirs, gx_mine, gx_theirs, dw_mine, dw_theirs = run_experts(
        shards, owners, x, g, weights, own_w
    )

    my_hit, my_rank = mine(hits), mine(ranks)
    other_hit, other_rank = other(hits), other(ranks)

    def by_block(kept, back):
        def take(part, hit, rank):
            chosen = part[jnp.clip(rank, 0, CAP - 1)]
            return jnp.where(hit[:, None, None, None] == 1, chosen.astype(jnp.float32), 0.0)

        total = take(kept, my_hit, my_rank) + take(back, other_hit, other_rank)
        total = total.astype(jnp.bfloat16).reshape(block_count, owners, block_len, width // owners)

        def chunk(step):
            return lax.dynamic_index_in_dim(total, owner ^ step, 1, keepdims=False)

        received = [exchange(chunk(step), step) for step in range(1, owners)]
        summed = chunk(0).astype(jnp.float32)
        for part in received:
            summed = summed + part.astype(jnp.float32)
        return summed.astype(jnp.bfloat16).reshape(block_count * block_len, width // owners)

    y_back, gx_back, dw_got = swap(y_theirs), swap(gx_theirs), swap(dw_theirs)
    mixed = by_block(y_mine, y_back)
    grad_tokens = by_block(gx_mine, gx_back)
    dw_kept = dw_mine
    dw_all = jnp.where(
        core == 0, jnp.stack([dw_kept, dw_got]), jnp.stack([dw_got, dw_kept])
    ).astype(jnp.float32)
    grad_w_in = jnp.transpose(dw_all[:, 0], (0, 2, 1))
    return (mixed, grad_tokens, grad_w_in, dw_all[:, 1])


def gelu_cdf(values):
    return 0.5 * (1.0 + jax.scipy.special.erf(values * 0.7071067811865476))


def gelu_slope(values):
    return gelu_cdf(values) + values * jnp.exp(-0.5 * values * values) * 0.3989422804014327


def place_rows(terms, blocks, block_count):
    block_len = terms.shape[-2]
    width = terms.shape[-1]
    zeros = jnp.zeros((block_count, block_len, width), jnp.float32)
    placed = zeros.at[blocks.reshape(-1)].add(terms.reshape(-1, block_len, width))
    return placed.reshape(block_count * block_len, width)


def plain_body(tokens, assign, gates, cot, w_in, w_out):
    own_count = w_in.shape[0]
    block_count = assign.shape[0]
    block_len = tokens.shape[0] // block_count
    width = tokens.shape[1]
    full_in, full_out = (
        lax.all_gather(w_in, "dp", axis=2, tiled=True),
        lax.all_gather(w_out, "dp", axis=1, tiled=True),
    )
    expert_ids = lax.axis_index("own") * own_count + jnp.arange(own_count, dtype=jnp.int32)
    blocks, is_valid = jax.vmap(pick_blocks, (None, 0, None))(assign, expert_ids, CAP)[:2]
    gate_blocks = gates.reshape(block_count, block_len, 2)
    mixing = jax.vmap(block_gates, (None, None, 0, 0, 0))(
        assign, gate_blocks, blocks, is_valid, expert_ids
    )
    weight_rows = mixing.reshape(own_count, CAP * block_len)
    token_blocks = tokens.reshape(block_count, block_len, width)
    picked = token_blocks[blocks].reshape(own_count, CAP * block_len, width)
    pre_act = jnp.einsum("erd,edf->erf", picked, full_in, preferred_element_type=jnp.float32)
    hidden = (pre_act * gelu_cdf(pre_act)).astype(jnp.bfloat16)
    expert_out = jnp.einsum("erf,efd->erd", hidden, full_out, preferred_element_type=jnp.float32)
    contrib = (weight_rows[..., None] * expert_out).reshape(own_count, CAP, block_len, width)
    partial_rows = place_rows(contrib, blocks, block_count)
    mixed = lax.psum_scatter(
        partial_rows.astype(jnp.bfloat16), "own", scatter_dimension=1, tiled=True
    )
    cot_full = lax.all_gather(cot, "own", axis=1, tiled=True)
    cot_picked = cot_full.reshape(block_count, block_len, width)[blocks].reshape(
        own_count, CAP * block_len, width
    )
    grad_out = (weight_rows[..., None] * cot_picked.astype(jnp.float32)).astype(jnp.bfloat16)
    grad_hidden = jnp.einsum("erd,efd->erf", grad_out, full_out, preferred_element_type=jnp.float32)
    grad_pre = (grad_hidden * gelu_slope(pre_act)).astype(jnp.bfloat16)
    grad_in_terms = jnp.einsum(
        "erf,edf->erd", grad_pre, full_in, preferred_element_type=jnp.float32
    )
    grad_rows = place_rows(
        grad_in_terms.reshape(own_count, CAP, block_len, width), blocks, block_count
    )
    grad_tokens = lax.psum_scatter(
        grad_rows.astype(jnp.bfloat16), "own", scatter_dimension=1, tiled=True
    )
    out_full = jnp.einsum("erf,erd->efd", hidden, grad_out, preferred_element_type=jnp.float32)
    in_full = jnp.einsum("erf,erd->efd", grad_pre, picked, preferred_element_type=jnp.float32)
    grad_w_out, in_shard = (
        lax.psum_scatter(
            out_full.astype(jnp.bfloat16), "dp", scatter_dimension=1, tiled=True
        ).astype(jnp.float32),
        lax.psum_scatter(
            in_full.astype(jnp.bfloat16), "dp", scatter_dimension=1, tiled=True
        ).astype(jnp.float32),
    )
    grad_w_in = jnp.transpose(in_shard, (0, 2, 1))
    return (mixed, grad_tokens, grad_w_in, grad_w_out)


def solution(mesh):
    placed = (
        P("dp", None),
        P("dp", None),
        P("dp", None),
        P("dp", "own"),
        P("own", None, "dp"),
        P("own", "dp", None),
    )
    return jax.shard_map(
        functools.partial(body, mesh.shape["dp"], mesh.shape["own"]),
        mesh=mesh,
        in_specs=placed,
        out_specs=(P("dp", "own"), P("dp", "own"), P("own", None, "dp"), P("own", "dp", None)),
        check_vma=False,
    )
```
